32 devices in a mesh: dp: 4 (over y, core), expert: 8 (over z, x).
Axes of the slice: x: 2, y: 2, z: 4, core: 2. Of those that a mesh axis runs over, the one named last changes fastest.
Arguments:
- tokens: bfloat16 [2, 8192, 768], P(None, ('dp', 'expert')), may hold values from -6 to 6
- gain_attn: float32 [768], replicated, may hold values from 0.25 to 1.75
- qkv_weight: bfloat16 [768, 2304], P(('dp', 'expert')), may hold values from -0.21875 to 0.21875
- out_weight: bfloat16 [768, 768], P(('dp', 'expert')), may hold values from -1.25 to 1.25
- bias_table: float32 [32, 12], replicated, may hold values from -4 to 4
- gain_ffn: float32 [768], replicated, may hold values from 0.25 to 1.75
- router_weight: bfloat16 [768, 16], P(('dp', 'expert')), may hold values from -0.14941406 to 0.14941406
- expert_in: bfloat16 [16, 768, 3072], P('expert', None, 'dp'), may hold values from -0.21875 to 0.21875
- expert_out: bfloat16 [16, 3072, 768], P('expert', 'dp'), may hold values from -0.15625 to 0.15625
- lengths: int32 [2, 32, 4], P(None, ('dp', 'expert')), may hold values from 1 to 160, 256 in all within a row
- buckets: int32 [256], replicated, may hold values from 0 to 31, as said below
- routes: int32 [2, 8192, 2], P(None, ('dp', 'expert')), may hold values from 0 to 15, all different within a row; in each aligned block of 256 rows (0 to 255, 256 to 511, ..., all dimensions but the last counted through in order) at most 48 rows name the same one
- cotangent: bfloat16 [2, 8192, 768], P(None, ('dp', 'expert')), may hold values from -6 to 6
Outputs:
- block_out: bfloat16 [2, 8192, 768], P(None, ('dp', 'expert'))
- tokens_grad: bfloat16 [2, 8192, 768], P(None, ('dp', 'expert'))
- gain_attn_grad: float32 [768], replicated
- qkv_grad: float32 [768, 2304], P(('dp', 'expert'))
- out_grad: float32 [768, 768], P(('dp', 'expert'))
- table_grad: float32 [32, 12], replicated
- gain_ffn_grad: float32 [768], replicated
- router_grad: float32 [768, 16], P(('dp', 'expert'))
- expert_in_grad: float32 [16, 768, 3072], P('expert', None, 'dp')
- expert_out_grad: float32 [16, 3072, 768], P('expert', 'dp')
The draws below stay inside these ranges and needn't reach their ends.
Inputs may be any that keep to these rules, and one draw needn't show every extreme that they name: The 4 lengths of each device's micro-batch sum to 256. `buckets`: Non-decreasing in the distance, 0 at distance 0 and 31 at the largest distance. `routes`: A token's two experts differ; in each micro-batch the 256 tokens of one device name one expert at most 48 times.
All inputs are finite; a program needn't handle non-finite values.
Results may differ from the reference program's by a relative error of at most 0.013.
Values may be sent and summed in bfloat16 or wider, within the bound.
A program may use at most 192 MiB of HBM per device.

```python
import math
import jax
import jax.numpy as jnp
import numpy as np
from jax import lax

D = 768
HEADS = 12
HEAD_DIM = 64
FF = 3072
NB = 32
MICRO = 2
TOK_MB = 256
SEQ_MB = 4
MAX_LEN = 160
EXPERTS = 16
SHARDS = 32
TOKENS = 8192
CAP = 48


def draw_buckets(key, part):
    key = jax.random.fold_in(key, 7)
    order = jax.random.permutation(key, TOK_MB - 1) + 1
    marks = jnp.zeros((TOK_MB,), jnp.int32).at[order[:NB - 1]].set(1)
    return jnp.cumsum(marks).astype(jnp.int32)


def steps_of(rng, extent, pieces, low, top_value):
    level = 1.0
    for axis_at, shards_of in pieces:
        draws = jax.random.uniform(jax.random.fold_in(jax.random.fold_in(rng, 6), axis_at), (shards_of,), jnp.float32, low / len(pieces), top_value / len(pieces))
        level = level * jnp.repeat(jnp.exp(draws), extent[axis_at] // shards_of).reshape((-1,) + (1,) * (len(extent) - 1 - axis_at))
    return level


def split_up(number_of, total, reach, skew):
    weights = [(1 << 20) // math.isqrt(rank ** skew) + 1 for rank in range(2, number_of + 1)]
    spare, holding = total - reach - (number_of - 1), [1] * (number_of - 1)
    while spare > 0:
        movable = [i for i in range(number_of - 1) if holding[i] < reach]
        pool, budget = sum([weights[i] for i in movable]), spare
        for i in movable:
            more = min(reach - holding[i], max(1, budget * weights[i] // pool), spare)
            holding[i] = holding[i] + more
            spare = spare - more
    return np.array([reach] + holding)


def uneven(stream_key, count, total, most, lean):
    if count == 2:
        one = jax.random.randint(stream_key, (), max(1, total - most), min(most, total - 1) + 1)
        return jnp.stack([one, total - one])
    sizes = jnp.asarray(split_up(count, total, most, lean), jnp.int32)
    couples = (count - 1) // 2
    donor, receiver = sizes[1:1 + 2 * couples:2], sizes[2:2 + 2 * couples:2]
    room = jnp.minimum(donor - 1, most - receiver)
    moved = jax.random.randint(jax.random.fold_in(stream_key, 1), (couples,), 0, 1 << 20) % (room + 1)
    sizes = sizes.at[1:1 + 2 * couples:2].set(donor - moved).at[2:2 + 2 * couples:2].set(receiver + moved)
    return sizes[jax.random.permutation(jax.random.fold_in(stream_key, 2), count)]


def deal_out(stream_key, own, number, rows, number_of, top, bound, slope):
    order = jax.random.permutation(stream_key, number_of)
    packed, common = portions_of(number_of, rows * top, bound, slope, True), portions_of(number_of, rows * top, bound, slope, False)
    places = jnp.arange(number_of)

    def named(sizes, rotation):
        used = int((sizes > 0).sum())
        fixed = max(1, used // 4)
        shifted = fixed + (places - fixed + rotation * (used - fixed)) % max(1, number_of - fixed)
        return jnp.zeros((number_of,), jnp.int32).at[order[jnp.where(places < fixed, places, shifted)]].set(jnp.asarray(sizes, jnp.int32))

    sizes = jnp.where(number % 4 == 0, named(packed, number // 4), named(common, number - number // 4 - 1))
    mixed = jax.random.permutation(jax.random.fold_in(own, 3), number_of)
    donor, receiver = mixed[0:number_of // 2 * 2:2], mixed[1:number_of // 2 * 2:2]
    slack = jnp.minimum(sizes[donor] - 1, bound - sizes[receiver]) // 2
    slack = jnp.where((donor == order[0]) | (receiver == order[0]) | (sizes[receiver] == 0), 0, jnp.maximum(slack, 0))
    shifted = jax.random.randint(jax.random.fold_in(own, 4), (number_of // 2,), 0, 1 << 20) % (slack + 1)
    sizes = sizes.at[donor].add(-shifted).at[receiver].add(shifted)
    members = jnp.searchsorted(jnp.cumsum(sizes), jnp.arange(rows * top), side="right").astype(jnp.int32)
    table = members.reshape(top, rows).T
    table = table[jax.random.permutation(jax.random.fold_in(own, 1), rows)]
    rotation = jax.random.randint(jax.random.fold_in(own, 2), (rows, 1), 0, top)
    return jnp.take_along_axis(table, (jnp.arange(top)[None, :] + rotation) % top, axis=1)


def portions_of(amount, total, limit, skew, full):
    loads = [(1 << 20) // math.isqrt(grade ** skew) + 1 for grade in range(1, amount + 1)]
    largest = limit if full else min(limit, max(-(-total // amount), total * loads[0] // sum(loads)))
    least = 1 if total - largest >= amount - 1 else 0
    given, spare = [largest] + [least] * (amount - 1), total - largest - least * (amount - 1)
    while spare > 0:
        free = [i for i in range(1, amount) if given[i] < largest] or [i for i in range(1, amount) if given[i] < limit]
        pool, left = sum([loads[i] for i in free]), spare
        for i in free:
            extra = min(limit - given[i], max(1, left * loads[i] // pool), spare)
            given[i] = given[i] + extra
            spare = spare - extra
    return np.array(given)


def scatter_about(rng, shape, width, most, pieces=(), held_as=jnp.bfloat16):
    values = jax.random.normal(rng, shape, jnp.float32) * width
    if len(pieces) > 0:
        values = steps_of(rng, shape, pieces, -0.22, 0.18) * values
    return jnp.clip(values, min=-most, max=most).astype(held_as)


def setup_inputs(seed: int = 0) -> dict:
    seeds = jax.random.split(jax.random.key(seed), 14)
    tokens = scatter_about(seeds[0], (MICRO, TOKENS, D), 1.0, 6.0, ((1, 32),))
    gain_attn = jnp.clip(1.0 + 0.15 * jax.random.normal(seeds[1], (D,), jnp.float32), 0.25, 1.75)
    qkv_weight = scatter_about(seeds[2], (D, 3 * D), D ** -0.5, 0.21875, ((0, 32),))
    out_weight = scatter_about(seeds[3], (D, D), (D // 32) ** -0.5, 1.25, ((0, 32),))
    bias_table = scatter_about(seeds[4], (NB, HEADS), 1.0, 4.0, (), jnp.float32)
    gain_ffn = jnp.clip(1.0 + 0.15 * jax.random.normal(seeds[5], (D,), jnp.float32), 0.25, 1.75)
    router_weight = scatter_about(seeds[6], (D, EXPERTS), 0.025, 0.14941406, ((0, 32),))
    expert_in = scatter_about(seeds[7], (EXPERTS, D, FF), D ** -0.5, 0.21875, ((0, 8), (2, 4)))
    expert_out = scatter_about(seeds[8], (EXPERTS, FF, D), (FF // 2) ** -0.5, 0.15625, ((0, 8), (1, 4)))
    lengths = jax.vmap(lambda own: uneven(own, SEQ_MB, TOK_MB, MAX_LEN, 1))(jax.random.split(seeds[9], MICRO * SHARDS)).reshape((MICRO, SHARDS, SEQ_MB)).astype(jnp.int32)
    buckets = draw_buckets(jax.random.fold_in(seeds[13], 71), 0)
    routes_keys = jax.random.split(jax.random.fold_in(seeds[11], 1), MICRO * TOKENS // TOK_MB)
    routes_turns = jax.random.permutation(jax.random.fold_in(seeds[11], 3), MICRO * TOKENS // TOK_MB)
    routes = jax.vmap(lambda own, number: deal_out(jax.random.fold_in(seeds[11], 2), own, number, TOK_MB, EXPERTS, 2, CAP, 1))(routes_keys, routes_turns).reshape((MICRO, TOKENS, 2))
    cotangent = scatter_about(seeds[12], (MICRO, TOKENS, D), 1.0, 6.0, ((1, 32),))
    return {"tokens": tokens, "gain_attn": gain_attn, "qkv_weight": qkv_weight, "out_weight": out_weight, "bias_table": bias_table, "gain_ffn": gain_ffn, "router_weight": router_weight, "expert_in": expert_in, "expert_out": expert_out, "lengths": lengths, "buckets": buckets, "routes": routes, "cotangent": cotangent}


@jax.custom_vjp
def low(v):
    return lax.optimization_barrier(v.astype(jnp.bfloat16)).astype(jnp.float32)

@jax.custom_vjp
def low_back(v):
    return v

def low_keep(v):
    return (low(v), None)

def low_pass(kept, grad):
    return (grad,)

def back_keep(v):
    return (v, None)

def back_low(kept, grad):
    return (low(grad),)
low.defvjp(low_keep, low_pass)
low_back.defvjp(back_keep, back_low)
HIGHEST = lax.Precision.HIGHEST
EPSILON = 1e-06

def rms_norm(values, gain_vec):
    return values * lax.rsqrt(lax.optimization_barrier(jnp.mean(values * values, axis=-1, keepdims=True)) + EPSILON) * gain_vec

def gelu_tanh(values):
    return jax.nn.gelu(values, approximate=True)

def segment_ids(length_row):
    seq_ends = jnp.cumsum(length_row)
    positions = jnp.arange(TOK_MB, dtype=jnp.int32)
    return lax.optimization_barrier(jnp.sum((positions[:, None] >= seq_ends[None, :]).astype(jnp.int32), axis=1))

def attend_block(qkv_block, length_row, bias_full):
    queries = qkv_block[:, :D].reshape(TOK_MB, HEADS, HEAD_DIM)
    key_rows = qkv_block[:, D:2 * D].reshape(TOK_MB, HEADS, HEAD_DIM)
    value_rows = qkv_block[:, 2 * D:].reshape(TOK_MB, HEADS, HEAD_DIM)
    segment = segment_ids(length_row)
    positions = jnp.arange(TOK_MB, dtype=jnp.int32)
    allowed = (positions[:, None] >= positions[None, :]) & (segment[:, None] == segment[None, :])
    scores = jnp.einsum('qhd,khd->hqk', queries, key_rows, precision=HIGHEST) * HEAD_DIM ** (-0.5) + bias_full
    scores = low_back(scores)
    scores = jnp.where(allowed[None], scores, -1e+30)
    probability = jax.nn.softmax(scores, axis=-1)
    context = jnp.einsum('hqk,khd->qhd', low(probability), value_rows, precision=HIGHEST)
    return context.reshape(TOK_MB, D)

def expert_apply(group):
    row_data, first_weight, second_weight = group
    pre_act = low_back(jnp.dot(row_data, first_weight, precision=HIGHEST, preferred_element_type=jnp.float32))
    hidden = low(gelu_tanh(pre_act))
    return low(low_back(jnp.dot(hidden, second_weight, precision=HIGHEST, preferred_element_type=jnp.float32)))

def dispatch_index(routes):
    block_count = routes.shape[0] * routes.shape[1] // TOK_MB
    route_rows = routes.reshape(block_count, TOK_MB * 2)
    expert_ids = jnp.arange(EXPERTS, dtype=jnp.int32)
    expert_hits = (route_rows[:, :, None] == expert_ids[None, None, :]).astype(jnp.int32)
    slot_rank = lax.optimization_barrier(jnp.sum((jnp.cumsum(expert_hits, axis=1) - 1) * expert_hits, axis=2))
    block_ids = jnp.arange(block_count, dtype=jnp.int32)[:, None]
    return ((route_rows * block_count + block_ids) * CAP + slot_rank).reshape(-1, 2)

def layer(tokens, gain_attn, qkv_weight, out_weight, bias_table, gain_ffn, router_weight, expert_in, expert_out, lengths, buckets, routes):
    block_count = MICRO * SHARDS
    normed = low(rms_norm(tokens, gain_attn))
    qkv = low(low_back(jnp.dot(normed.reshape(-1, D), qkv_weight, precision=HIGHEST, preferred_element_type=jnp.float32)))
    positions = jnp.arange(TOK_MB, dtype=jnp.int32)
    distance = jnp.maximum(positions[:, None] - positions[None, :], 0)
    bias_full = jnp.transpose(bias_table[buckets[distance]], (2, 0, 1))

    def one_block(group):
        return attend_block(group[0], group[1], bias_full)
    context = lax.map(jax.checkpoint(one_block), (qkv.reshape(block_count, TOK_MB, 3 * D), lengths.reshape(block_count, SEQ_MB)))
    context = low(low_back(context.reshape(-1, D)))
    attention = low_back(jnp.dot(context, out_weight, precision=HIGHEST, preferred_element_type=jnp.float32))
    middle = tokens + attention.reshape(tokens.shape)
    ffn_in = low(rms_norm(middle, gain_ffn)).reshape(-1, D)
    logits = low_back(jnp.dot(ffn_in, router_weight, precision=HIGHEST, preferred_element_type=jnp.float32))
    route_pairs = routes.reshape(-1, 2)
    chosen = jnp.take_along_axis(logits, route_pairs, axis=1)
    gate_weights = jax.nn.softmax(chosen, axis=-1)
    slot_index = dispatch_index(routes).reshape(-1)
    copies = jnp.repeat(ffn_in, 2, axis=0)
    buffer = jnp.zeros((EXPERTS * block_count * CAP, D), jnp.float32).at[slot_index].set(copies)
    buffer = low_back(buffer).reshape(EXPERTS, block_count * CAP, D)
    produced = lax.map(jax.checkpoint(expert_apply), (buffer, expert_in, expert_out))
    returned = produced.reshape(-1, D)[slot_index].reshape(-1, 2, D)
    mixture = lax.optimization_barrier(jnp.sum(gate_weights[:, :, None] * returned, axis=1))
    return middle + mixture.reshape(tokens.shape)

def reference(tokens, gain_attn, qkv_weight, out_weight, bias_table, gain_ffn, router_weight, expert_in, expert_out, lengths, buckets, routes, cotangent):
    floats = (tokens.astype(jnp.float32), gain_attn.astype(jnp.float32), qkv_weight.astype(jnp.float32), out_weight.astype(jnp.float32), bias_table.astype(jnp.float32), gain_ffn.astype(jnp.float32), router_weight.astype(jnp.float32), expert_in.astype(jnp.float32), expert_out.astype(jnp.float32))

    def forward(*values):
        return layer(*values, lengths, buckets, routes)
    result, pullback = jax.vjp(forward, *floats)
    gradients = pullback(cotangent.astype(jnp.float32))
    return (result.astype(jnp.bfloat16), gradients[0].astype(jnp.bfloat16), gradients[1], gradients[2], gradients[3], gradients[4], gradients[5], gradients[6], gradients[7], gradients[8])
```

```python
import functools

import jax
import jax.numpy as jnp
from jax import lax
from jax.sharding import PartitionSpec as P

EPSILON = 1e-06
HIGHEST = lax.Precision.HIGHEST


def rms_norm(values, gain_vec):
    return (
        values * lax.rsqrt(jnp.mean(values * values, axis=-1, keepdims=True) + EPSILON) * gain_vec
    )


def gelu_tanh(values):
    return jax.nn.gelu(values, approximate=True)


def attention_scores(queries, key_rows, bias_full, allowed, score_scale):
    scores = (
        jnp.einsum("mqhd,mkhd->mhqk", queries, key_rows, preferred_element_type=jnp.float32)
        * score_scale
        + bias_full[None]
    )
    return jnp.where(allowed[:, None], scores, -1e30)


def flip_pairs(size, bit):
    return [(i, i ^ bit) for i in range(size)]


def bits_of(size):
    return [1 << i for i in range(size.bit_length() - 1)]


def gather_relative(block, size):
    blocks = [block]
    for bit in reversed(bits_of(size)):
        blocks = blocks + [lax.ppermute(b, "dp", flip_pairs(size, bit)) for b in blocks]
    return blocks


def scatter_relative(parts, size):
    for bit in bits_of(size):
        half = len(parts) // 2
        arrived = [
            lax.ppermute(p.astype(jnp.bfloat16), "dp", flip_pairs(size, bit)) for p in parts[half:]
        ]
        parts = [p.astype(jnp.float32) + q.astype(jnp.float32) for p, q in zip(parts[:half], arrived)]
    return parts[0]


def halving_scatter(matrix, sizes, order):
    axis_bits = [("dp", b) for b in reversed(bits_of(sizes["dp"]))]
    axis_bits += [("expert", b) for b in reversed(bits_of(sizes["expert"]))]
    blocks = sizes["dp"] * sizes["expert"]
    rows, columns = matrix.shape
    held = matrix.reshape((2,) * len(axis_bits) + (rows // blocks, columns))
    left = list(axis_bits)
    for axis, bit in order:
        place = left.index((axis, bit))
        left.pop(place)
        mine = (lax.axis_index(axis) // bit) % 2
        keep = lax.dynamic_index_in_dim(held, mine, place, keepdims=False)
        send = lax.dynamic_index_in_dim(held, 1 - mine, place, keepdims=False)
        arrived = lax.ppermute(send.astype(jnp.bfloat16), axis, flip_pairs(sizes[axis], bit))
        held = keep.astype(jnp.float32) + arrived.astype(jnp.float32)
    return held


def butterfly_sum(values, sizes):
    for axis in ("dp", "expert"):
        for bit in bits_of(sizes[axis]):
            values = values + lax.ppermute(values, axis, flip_pairs(sizes[axis], bit))
    return values


def gelu_slope(values, upstream):
    return jax.vjp(gelu_tanh, values)[1](upstream)[0]


def dot_nn(a, b):
    return lax.dot_general(a, b, (((1,), (0,)), ((), ())), preferred_element_type=jnp.float32)


def dot_nt(a, b):
    return lax.dot_general(a, b, (((1,), (1,)), ((), ())), preferred_element_type=jnp.float32)


def dot_tn(a, b):
    return lax.dot_general(a, b, (((0,), (0,)), ((), ())), preferred_element_type=jnp.float32)


def on_device(
    sizes,
    tokens,
    gain_attn,
    qkv_weight,
    out_weight,
    bias_table,
    gain_ffn,
    router_weight,
    expert_in,
    expert_out,
    lengths,
    buckets,
    routes,
    cotangent,
):
    micro, tok_mb, model_width = tokens.shape
    experts = router_weight.shape[1]
    capacity = 3 * tok_mb // experts
    bucket_count, head_count = bias_table.shape
    head_size = model_width // head_count
    score_scale = head_size ** (-0.5)
    row_count = micro * tok_mb
    local_experts = experts // sizes["expert"]
    orders = (
        [("dp", 1), ("expert", 1)]
        + [("dp", b) for b in reversed(bits_of(sizes["dp"])) if b > 1]
        + [("expert", b) for b in reversed(bits_of(sizes["expert"])) if b > 1],
        [("dp", 1)]
        + [("dp", b) for b in reversed(bits_of(sizes["dp"])) if b > 1]
        + [("expert", 1)]
        + [("expert", b) for b in reversed(bits_of(sizes["expert"])) if b > 1],
    )
    packed = jnp.concatenate(
        [qkv_weight, out_weight, jnp.pad(router_weight, ((0, 0), (0, -experts % 128)))], axis=1
    )
    packed_full = lax.all_gather(packed, ("dp", "expert"), axis=0, tiled=True)
    qkv_full = packed_full[:, : 3 * model_width]
    out_full = packed_full[:, 3 * model_width : 4 * model_width]
    router_full = packed_full[:, 4 * model_width : 4 * model_width + experts]
    in_blocks = gather_relative(expert_in, sizes["dp"])
    back_blocks = gather_relative(expert_out, sizes["dp"])
    flat_x = tokens.astype(jnp.float32).reshape(row_count, model_width)
    normed_low = rms_norm(flat_x, gain_attn).astype(jnp.bfloat16)
    qkv_act = jnp.dot(normed_low, qkv_full, preferred_element_type=jnp.float32).astype(jnp.bfloat16)
    queries = qkv_act[:, :model_width].reshape(micro, tok_mb, head_count, head_size)
    key_rows = qkv_act[:, model_width : 2 * model_width].reshape(
        micro, tok_mb, head_count, head_size
    )
    value_rows = qkv_act[:, 2 * model_width :].reshape(micro, tok_mb, head_count, head_size)
    positions = jnp.arange(tok_mb, dtype=jnp.int32)
    seq_ends = jnp.cumsum(lengths[:, 0, :], axis=1)
    segment = jnp.sum((positions[None, :, None] >= seq_ends[:, None, :]).astype(jnp.int32), axis=2)
    allowed = (positions[:, None] >= positions[None, :])[None] & (
        segment[:, :, None] == segment[:, None, :]
    )
    distance = jnp.maximum(positions[:, None] - positions[None, :], 0)
    bucket_ids = jnp.arange(bucket_count, dtype=jnp.int32)
    thresholds = jnp.sum((buckets[None, :] < bucket_ids[:, None]).astype(jnp.int32), axis=1)
    distance_bucket = jnp.sum(
        (distance[:, :, None] >= thresholds[1:][None, None, :]).astype(jnp.int32), axis=2
    )
    bucket_hot = (distance_bucket[:, :, None] == bucket_ids).astype(jnp.float32)
    bias_full = jnp.einsum("qkb,bh->hqk", bucket_hot, bias_table, precision=HIGHEST)
    scores = attention_scores(queries, key_rows, bias_full, allowed, score_scale)
    row_max = jnp.max(scores, axis=-1, keepdims=True)
    row_sum = jnp.sum(jnp.exp(scores - row_max), axis=-1, keepdims=True)
    log_total = row_max + jnp.log(row_sum)
    probability = jnp.exp(scores - log_total)
    context = jnp.einsum(
        "mhqk,mkhd->mqhd",
        probability.astype(jnp.bfloat16),
        value_rows,
        preferred_element_type=jnp.float32,
    )
    context = context.reshape(row_count, model_width).astype(jnp.bfloat16)
    middle = flat_x + jnp.dot(context, out_full, preferred_element_type=jnp.float32)
    ffn_low = rms_norm(middle, gain_ffn).astype(jnp.bfloat16)
    logits = jnp.dot(ffn_low, router_full, preferred_element_type=jnp.float32)
    grad_out = cotangent.astype(jnp.float32).reshape(row_count, model_width)
    expert_ids = jnp.arange(experts, dtype=jnp.int32)
    flat_routes = routes.reshape(row_count, 2)
    route_hot = (flat_routes[:, :, None] == expert_ids).astype(jnp.float32)
    token_hits = jnp.sum(route_hot, axis=1)
    chosen = jnp.sum(route_hot * logits[:, None, :], axis=2)
    gate_weights = jax.nn.softmax(chosen, axis=-1)
    rows_at = jnp.arange(row_count, dtype=jnp.int32)
    micro_at = rows_at // tok_mb
    before = (
        (rows_at[None, :] < rows_at[:, None]) & (micro_at[None, :] == micro_at[:, None])
    ).astype(jnp.bfloat16)
    earlier = jnp.dot(before, token_hits.astype(jnp.bfloat16), preferred_element_type=jnp.float32)
    rank = jnp.sum(route_hot * earlier[:, None, :], axis=2).astype(jnp.int32)
    group_rows = micro * capacity
    slot_rows = sizes["expert"] * group_rows
    column = (
        (flat_routes % local_experts) * slot_rows
        + (flat_routes // local_experts) * group_rows
        + micro_at[:, None] * capacity
        + rank
    )
    columns_at = jnp.arange(local_experts * slot_rows, dtype=jnp.int32)
    first_hot = column[:, 0:1] == columns_at[None, :]
    second_hot = column[:, 1:2] == columns_at[None, :]
    slot_hot = (first_hot | second_hot).astype(jnp.bfloat16)
    gated_hot = jnp.where(
        first_hot, gate_weights[:, 0:1], jnp.where(second_hot, gate_weights[:, 1:2], 0.0)
    ).astype(jnp.bfloat16)
    cotangent_rows = cotangent.reshape(row_count, model_width)

    def exchange(values):
        sent = values.reshape((sizes["expert"], group_rows) + values.shape[1:])
        got = lax.all_to_all(sent, "expert", split_axis=0, concat_axis=0, tiled=True)
        return got.reshape(values.shape)

    spans = [slice(e * slot_rows, (e + 1) * slot_rows) for e in range(local_experts)]
    received, grad_recv = [], []
    for span in spans:
        received.append(exchange(dot_tn(slot_hot[:, span], ffn_low).astype(jnp.bfloat16)))
        grad_recv.append(
            exchange(dot_tn(gated_hot[:, span], cotangent_rows).astype(jnp.bfloat16))
        )
    produced, grad_back, gate_terms, in_grads, out_grads = [], [], [], [], []
    for e in range(local_experts):
        in_full = jnp.concatenate([b[e] for b in in_blocks], axis=1)
        back_full = jnp.concatenate([b[e] for b in back_blocks], axis=0)
        block_width = expert_in.shape[2]
        pre_act = dot_nn(received[e], in_full)
        hidden = gelu_tanh(pre_act).astype(jnp.bfloat16)
        made = dot_nn(hidden, back_full).astype(jnp.bfloat16)
        gate_terms.append(
            jnp.sum(grad_recv[e].astype(jnp.float32) * made.astype(jnp.float32), axis=1)
        )
        grad_pre = gelu_slope(pre_act, dot_nt(grad_recv[e], back_full)).astype(jnp.bfloat16)
        grad_rows = dot_nt(grad_pre, in_full).astype(jnp.bfloat16)
        grad_back.append(exchange(grad_rows))
        produced.append(made)
        cuts = [slice(r * block_width, (r + 1) * block_width) for r in range(sizes["dp"])]
        out_grads.append(
            scatter_relative([dot_tn(hidden[:, c], grad_recv[e]) for c in cuts], sizes["dp"])
        )
        in_grads.append(
            scatter_relative([dot_tn(received[e], grad_pre[:, c]) for c in cuts], sizes["dp"])
        )
    expert_in_grad = jnp.stack(in_grads)
    expert_out_grad = jnp.stack(out_grads)
    terms = jnp.stack([t.reshape(sizes["expert"], group_rows) for t in gate_terms], axis=1)
    terms = lax.all_to_all(terms, "expert", split_axis=0, concat_axis=0, tiled=True)
    terms = jnp.transpose(terms, (1, 0, 2)).reshape(1, local_experts * slot_rows)
    returned = [exchange(made) for made in produced]
    mixture = sum(dot_nn(gated_hot[:, s], r) for s, r in zip(spans, returned))
    block_out = (middle + mixture).astype(jnp.bfloat16).reshape(tokens.shape)
    grad_ffn = sum(dot_nn(slot_hot[:, s], r) for s, r in zip(spans, grad_back))
    first_term = jnp.sum(jnp.where(first_hot, terms, 0.0), axis=1, keepdims=True)
    second_term = jnp.sum(jnp.where(second_hot, terms, 0.0), axis=1, keepdims=True)
    lean = gate_weights[:, 1:2] * first_term - gate_weights[:, 0:1] * second_term
    grad_logits = (lean * (route_hot[:, 0] - route_hot[:, 1])).astype(jnp.bfloat16)
    router_part = dot_tn(ffn_low, grad_logits)
    grad_ffn = grad_ffn + dot_nt(grad_logits, router_full)
    grad_mid_part, gain_ffn_part = jax.vjp(rms_norm, middle, gain_ffn)[1](grad_ffn)
    grad_middle = grad_out + grad_mid_part
    grad_attn = grad_middle.astype(jnp.bfloat16)
    out_part = jnp.einsum("nc,nd->cd", context, grad_attn, preferred_element_type=jnp.float32)
    grad_context = jnp.einsum(
        "nd,cd->nc", grad_attn, out_full, preferred_element_type=jnp.float32
    ).astype(jnp.bfloat16)
    grad_context = grad_context.reshape(micro, tok_mb, head_count, head_size)
    scores_again = attention_scores(queries, key_rows, bias_full, allowed, score_scale)
    prob_again = jnp.exp(scores_again - log_total)
    grad_prob = jnp.einsum(
        "mqhd,mkhd->mhqk", grad_context, value_rows, preferred_element_type=jnp.float32
    )
    row_delta = jnp.sum(prob_again * grad_prob, axis=-1, keepdims=True)
    grad_scores = (prob_again * (grad_prob - row_delta)).astype(jnp.bfloat16)
    score_total = jnp.sum(grad_scores.astype(jnp.float32), axis=0)
    table_part = jnp.einsum("hqk,qkb->bh", score_total, bucket_hot, precision=HIGHEST)
    grad_queries = (
        jnp.einsum("mhqk,mkhd->mqhd", grad_scores, key_rows, preferred_element_type=jnp.float32)
        * score_scale
    )
    grad_keys = (
        jnp.einsum("mhqk,mqhd->mkhd", grad_scores, queries, preferred_element_type=jnp.float32)
        * score_scale
    )
    grad_values = jnp.einsum(
        "mhqk,mqhd->mkhd",
        prob_again.astype(jnp.bfloat16),
        grad_context,
        preferred_element_type=jnp.float32,
    )
    grad_qkv = jnp.concatenate(
        [
            grad_queries.reshape(row_count, model_width),
            grad_keys.reshape(row_count, model_width),
            grad_values.reshape(row_count, model_width),
        ],
        axis=1,
    ).astype(jnp.bfloat16)
    qkv_part = jnp.einsum("nc,nd->cd", normed_low, grad_qkv, preferred_element_type=jnp.float32)
    grad_normed = jnp.einsum("nd,cd->nc", grad_qkv, qkv_full, preferred_element_type=jnp.float32)
    grad_x_part, gain_attn_part = jax.vjp(rms_norm, flat_x, gain_attn)[1](grad_normed)
    tokens_grad = (grad_middle + grad_x_part).astype(jnp.bfloat16).reshape(tokens.shape)
    split = 3 * model_width // 2
    early = halving_scatter(jnp.concatenate([out_part, router_part], axis=1), sizes, orders[0])
    out_grad, router_grad = early[:, :model_width], early[:, model_width:]
    qkv_grad = jnp.concatenate(
        [
            halving_scatter(qkv_part[:, :split], sizes, orders[0]),
            halving_scatter(qkv_part[:, split:], sizes, orders[1]),
        ],
        axis=1,
    )
    small = butterfly_sum(
        jnp.concatenate([gain_attn_part, gain_ffn_part, table_part.reshape(-1)]), sizes
    )
    gain_attn_grad = small[:model_width]
    gain_ffn_grad = small[model_width : 2 * model_width]
    table_grad = small[2 * model_width :].reshape(bias_table.shape)
    return (
        block_out,
        tokens_grad,
        gain_attn_grad,
        qkv_grad,
        out_grad,
        table_grad,
        gain_ffn_grad,
        router_grad,
        expert_in_grad,
        expert_out_grad,
    )


def solution(mesh):
    sizes = {"dp": mesh.shape["dp"], "expert": mesh.shape["expert"]}
    return jax.shard_map(
        functools.partial(on_device, sizes),
        mesh=mesh,
        in_specs=(
            P(None, ("dp", "expert"), None),
            P(),
            P(("dp", "expert"), None),
            P(("dp", "expert"), None),
            P(),
            P(),
            P(("dp", "expert"), None),
            P("expert", None, "dp"),
            P("expert", "dp", None),
            P(None, ("dp", "expert"), None),
            P(),
            P(None, ("dp", "expert"), None),
            P(None, ("dp", "expert"), None),
        ),
        out_specs=(
            P(None, ("dp", "expert"), None),
            P(None, ("dp", "expert"), None),
            P(),
            P(("dp", "expert"), None),
            P(("dp", "expert"), None),
            P(),
            P(),
            P(("dp", "expert"), None),
            P("expert", None, "dp"),
            P("expert", "dp", None),
        ),
        check_vma=False,
    )
```

```python
import functools

import jax
import jax.numpy as jnp
from jax import lax
from jax.sharding import PartitionSpec as P

EPSILON = 1e-06
HIGHEST = lax.Precision.HIGHEST


def rms_norm(values, gain_vec):
    return (
        values * lax.rsqrt(jnp.mean(values * values, axis=-1, keepdims=True) + EPSILON) * gain_vec
    )


def gelu_tanh(values):
    return jax.nn.gelu(values, approximate=True)


def attention_scores(queries, key_rows, bias_full, allowed, score_scale):
    scores = (
        jnp.einsum("mqhd,mkhd->mhqk", queries, key_rows, preferred_element_type=jnp.float32)
        * score_scale
        + bias_full[None]
    )
    return jnp.where(allowed[:, None], scores, -1e30)


def flip_pairs(size, bit):
    return [(i, i ^ bit) for i in range(size)]


def bits_of(size):
    return [1 << i for i in range(size.bit_length() - 1)]


def gather_far(block, size):
    blocks = [block]
    for bit in reversed(bits_of(size)[1:]):
        blocks = blocks + [lax.ppermute(b, "dp", flip_pairs(size, bit)) for b in blocks]
    return blocks


def gather_near(blocks, size):
    return blocks + [lax.ppermute(b, "dp", flip_pairs(size, 1)) for b in blocks]


def scatter_near(parts, size):
    half = len(parts) // 2
    arrived = [
        lax.ppermute(p.astype(jnp.bfloat16), "dp", flip_pairs(size, 1)) for p in parts[half:]
    ]
    return [p.astype(jnp.float32) + q.astype(jnp.float32) for p, q in zip(parts[:half], arrived)]


def scatter_far(parts, size):
    for bit in bits_of(size)[1:]:
        half = len(parts) // 2
        arrived = [
            lax.ppermute(p.astype(jnp.bfloat16), "dp", flip_pairs(size, bit)) for p in parts[half:]
        ]
        parts = [
            p.astype(jnp.float32) + q.astype(jnp.float32) for p, q in zip(parts[:half], arrived)
        ]
    return parts[0]


def halving_scatter(matrix, sizes, order):
    axis_bits = [("dp", b) for b in reversed(bits_of(sizes["dp"]))]
    axis_bits += [("expert", b) for b in reversed(bits_of(sizes["expert"]))]
    blocks = sizes["dp"] * sizes["expert"]
    rows, columns = matrix.shape
    held = matrix.reshape((2,) * len(axis_bits) + (rows // blocks, columns))
    left = list(axis_bits)
    for axis, bit in order:
        place = left.index((axis, bit))
        left.pop(place)
        mine = (lax.axis_index(axis) // bit) % 2
        keep = lax.dynamic_index_in_dim(held, mine, place, keepdims=False)
        send = lax.dynamic_index_in_dim(held, 1 - mine, place, keepdims=False)
        arrived = lax.ppermute(send.astype(jnp.bfloat16), axis, flip_pairs(sizes[axis], bit))
        held = keep.astype(jnp.float32) + arrived.astype(jnp.float32)
    return held


def butterfly_sum(values, sizes):
    for axis in ("dp", "expert"):
        for bit in bits_of(sizes[axis]):
            values = values + lax.ppermute(values, axis, flip_pairs(sizes[axis], bit))
    return values


def gelu_slope(values, upstream):
    return jax.vjp(gelu_tanh, values)[1](upstream)[0]


def dot_nn(a, b):
    return lax.dot_general(a, b, (((1,), (0,)), ((), ())), preferred_element_type=jnp.float32)


def dot_nt(a, b):
    return lax.dot_general(a, b, (((1,), (1,)), ((), ())), preferred_element_type=jnp.float32)


def dot_tn(a, b):
    return lax.dot_general(a, b, (((0,), (0,)), ((), ())), preferred_element_type=jnp.float32)


def on_device(
    sizes,
    tokens,
    gain_attn,
    qkv_weight,
    out_weight,
    bias_table,
    gain_ffn,
    router_weight,
    expert_in,
    expert_out,
    lengths,
    buckets,
    routes,
    cotangent,
):
    micro, tok_mb, model_width = tokens.shape
    experts = router_weight.shape[1]
    capacity = 3 * tok_mb // experts
    bucket_count, head_count = bias_table.shape
    head_size = model_width // head_count
    score_scale = head_size ** (-0.5)
    row_count = micro * tok_mb
    local_experts = experts // sizes["expert"]
    orders = (
        [("dp", 1), ("expert", 1)]
        + [("dp", b) for b in reversed(bits_of(sizes["dp"])) if b > 1]
        + [("expert", b) for b in reversed(bits_of(sizes["expert"])) if b > 1],
        [("dp", 1)]
        + [("dp", b) for b in reversed(bits_of(sizes["dp"])) if b > 1]
        + [("expert", 1)]
        + [("expert", b) for b in reversed(bits_of(sizes["expert"])) if b > 1],
    )
    packed = jnp.concatenate(
        [qkv_weight, out_weight, jnp.pad(router_weight, ((0, 0), (0, -experts % 128)))], axis=1
    )
    packed_full = lax.all_gather(packed, ("dp", "expert"), axis=0, tiled=True)
    qkv_full = packed_full[:, : 3 * model_width]
    out_full = packed_full[:, 3 * model_width : 4 * model_width]
    router_full = packed_full[:, 4 * model_width : 4 * model_width + experts]
    far_blocks = [
        gather_far(weight[e], sizes["dp"])
        for e in range(local_experts)
        for weight in (expert_in, expert_out)
    ]
    flat_x = tokens.astype(jnp.float32).reshape(row_count, model_width)
    normed_low = rms_norm(flat_x, gain_attn).astype(jnp.bfloat16)
    qkv_act = jnp.dot(normed_low, qkv_full, preferred_element_type=jnp.float32).astype(jnp.bfloat16)
    queries = qkv_act[:, :model_width].reshape(micro, tok_mb, head_count, head_size)
    key_rows = qkv_act[:, model_width : 2 * model_width].reshape(
        micro, tok_mb, head_count, head_size
    )
    value_rows = qkv_act[:, 2 * model_width :].reshape(micro, tok_mb, head_count, head_size)
    positions = jnp.arange(tok_mb, dtype=jnp.int32)
    seq_ends = jnp.cumsum(lengths[:, 0, :], axis=1)
    segment = jnp.sum((positions[None, :, None] >= seq_ends[:, None, :]).astype(jnp.int32), axis=2)
    allowed = (positions[:, None] >= positions[None, :])[None] & (
        segment[:, :, None] == segment[:, None, :]
    )
    distance = jnp.maximum(positions[:, None] - positions[None, :], 0)
    bucket_ids = jnp.arange(bucket_count, dtype=jnp.int32)
    thresholds = jnp.sum((buckets[None, :] < bucket_ids[:, None]).astype(jnp.int32), axis=1)
    distance_bucket = jnp.sum(
        (distance[:, :, None] >= thresholds[1:][None, None, :]).astype(jnp.int32), axis=2
    )
    bucket_hot = (distance_bucket[:, :, None] == bucket_ids).astype(jnp.float32)
    bias_full = jnp.einsum("qkb,bh->hqk", bucket_hot, bias_table, precision=HIGHEST)
    scores = attention_scores(queries, key_rows, bias_full, allowed, score_scale)
    row_max = jnp.max(scores, axis=-1, keepdims=True)
    row_sum = jnp.sum(jnp.exp(scores - row_max), axis=-1, keepdims=True)
    log_total = row_max + jnp.log(row_sum)
    probability = jnp.exp(scores - log_total)
    context = jnp.einsum(
        "mhqk,mkhd->mqhd",
        probability.astype(jnp.bfloat16),
        value_rows,
        preferred_element_type=jnp.float32,
    )
    context = context.reshape(row_count, model_width).astype(jnp.bfloat16)
    far_blocks = lax.optimization_barrier((far_blocks, context))[0]
    near_blocks = [gather_near(blocks, sizes["dp"]) for blocks in far_blocks]
    in_blocks, back_blocks = near_blocks[0::2], near_blocks[1::2]
    middle = flat_x + jnp.dot(context, out_full, preferred_element_type=jnp.float32)
    ffn_low = rms_norm(middle, gain_ffn).astype(jnp.bfloat16)
    logits = jnp.dot(ffn_low, router_full, preferred_element_type=jnp.float32)
    grad_out = cotangent.astype(jnp.float32).reshape(row_count, model_width)
    expert_ids = jnp.arange(experts, dtype=jnp.int32)
    flat_routes = routes.reshape(row_count, 2)
    route_hot = (flat_routes[:, :, None] == expert_ids).astype(jnp.float32)
    token_hits = jnp.sum(route_hot, axis=1)
    chosen = jnp.sum(route_hot * logits[:, None, :], axis=2)
    gate_weights = jax.nn.softmax(chosen, axis=-1)
    rows_at = jnp.arange(row_count, dtype=jnp.int32)
    micro_at = rows_at // tok_mb
    before = (
        (rows_at[None, :] < rows_at[:, None]) & (micro_at[None, :] == micro_at[:, None])
    ).astype(jnp.bfloat16)
    earlier = jnp.dot(before, token_hits.astype(jnp.bfloat16), preferred_element_type=jnp.float32)
    rank = jnp.sum(route_hot * earlier[:, None, :], axis=2).astype(jnp.int32)
    group_rows = micro * capacity
    slot_rows = sizes["expert"] * group_rows
    column = (
        (flat_routes % local_experts) * slot_rows
        + (flat_routes // local_experts) * group_rows
        + micro_at[:, None] * capacity
        + rank
    )
    columns_at = jnp.arange(local_experts * slot_rows, dtype=jnp.int32)
    first_hot = column[:, 0:1] == columns_at[None, :]
    second_hot = column[:, 1:2] == columns_at[None, :]
    slot_hot = (first_hot | second_hot).astype(jnp.bfloat16)
    gated_hot = jnp.where(
        first_hot, gate_weights[:, 0:1], jnp.where(second_hot, gate_weights[:, 1:2], 0.0)
    ).astype(jnp.bfloat16)
    cotangent_rows = cotangent.reshape(row_count, model_width)

    def exchange(values):
        sent = values.reshape((sizes["expert"], group_rows) + values.shape[1:])
        got = lax.all_to_all(sent, "expert", split_axis=0, concat_axis=0, tiled=True)
        return got.reshape(values.shape)

    spans = [slice(e * slot_rows, (e + 1) * slot_rows) for e in range(local_experts)]
    received, grad_recv = [], []
    for span in spans:
        received.append(exchange(dot_tn(slot_hot[:, span], ffn_low).astype(jnp.bfloat16)))
        grad_recv.append(
            exchange(dot_tn(gated_hot[:, span], cotangent_rows).astype(jnp.bfloat16))
        )
    produced, grad_back, gate_terms, in_grads, out_grads = [], [], [], [], []
    for e in range(local_experts):
        in_full = jnp.concatenate(in_blocks[e], axis=1)
        back_full = jnp.concatenate(back_blocks[e], axis=0)
        block_width = expert_in.shape[2]
        pre_act = dot_nn(received[e], in_full)
        hidden = gelu_tanh(pre_act).astype(jnp.bfloat16)
        made = dot_nn(hidden, back_full).astype(jnp.bfloat16)
        gate_terms.append(
            jnp.sum(grad_recv[e].astype(jnp.float32) * made.astype(jnp.float32), axis=1)
        )
        grad_pre = gelu_slope(pre_act, dot_nt(grad_recv[e], back_full)).astype(jnp.bfloat16)
        grad_rows = dot_nt(grad_pre, in_full).astype(jnp.bfloat16)
        grad_back.append(exchange(grad_rows))
        produced.append(made)
        cuts = [slice(r * block_width, (r + 1) * block_width) for r in range(sizes["dp"])]
        out_grads.append(
            scatter_near([dot_tn(hidden[:, c], grad_recv[e]) for c in cuts], sizes["dp"])
        )
        in_grads.append(
            scatter_near([dot_tn(received[e], grad_pre[:, c]) for c in cuts], sizes["dp"])
        )
    out_grads, in_grads, grad_back = lax.optimization_barrier((
        [[p[0]] + [q.astype(jnp.bfloat16) for q in p[1:]] for p in out_grads],
        [[p[0]] + [q.astype(jnp.bfloat16) for q in p[1:]] for p in in_grads],
        grad_back,
    ))
    out_grads = [scatter_far(parts, sizes["dp"]) for parts in out_grads]
    in_grads = [scatter_far(parts, sizes["dp"]) for parts in in_grads]
    terms = jnp.stack([t.reshape(sizes["expert"], group_rows) for t in gate_terms], axis=1)
    terms = lax.all_to_all(terms, "expert", split_axis=0, concat_axis=0, tiled=True)
    terms = jnp.transpose(terms, (1, 0, 2)).reshape(1, local_experts * slot_rows)
    returned = [exchange(made) for made in produced]
    mixture = sum(dot_nn(gated_hot[:, s], r) for s, r in zip(spans, returned))
    block_out = (middle + mixture).astype(jnp.bfloat16).reshape(tokens.shape)
    grad_ffn = sum(dot_nn(slot_hot[:, s], r) for s, r in zip(spans, grad_back))
    first_term = jnp.sum(jnp.where(first_hot, terms, 0.0), axis=1, keepdims=True)
    second_term = jnp.sum(jnp.where(second_hot, terms, 0.0), axis=1, keepdims=True)
    lean = gate_weights[:, 1:2] * first_term - gate_weights[:, 0:1] * second_term
    grad_logits = (lean * (route_hot[:, 0] - route_hot[:, 1])).astype(jnp.bfloat16)
    router_part = dot_tn(ffn_low, grad_logits)
    grad_ffn = grad_ffn + dot_nt(grad_logits, router_full)
    grad_mid_part, gain_ffn_part = jax.vjp(rms_norm, middle, gain_ffn)[1](grad_ffn)
    grad_middle = grad_out + grad_mid_part
    grad_attn = grad_middle.astype(jnp.bfloat16)
    out_part = jnp.einsum("nc,nd->cd", context, grad_attn, preferred_element_type=jnp.float32)
    grad_context = jnp.einsum(
        "nd,cd->nc", grad_attn, out_full, preferred_element_type=jnp.float32
    ).astype(jnp.bfloat16)
    grad_context = grad_context.reshape(micro, tok_mb, head_count, head_size)
    scores_again = attention_scores(queries, key_rows, bias_full, allowed, score_scale)
    prob_again = jnp.exp(scores_again - log_total)
    grad_prob = jnp.einsum(
        "mqhd,mkhd->mhqk", grad_context, value_rows, preferred_element_type=jnp.float32
    )
    row_delta = jnp.sum(prob_again * grad_prob, axis=-1, keepdims=True)
    grad_scores = (prob_again * (grad_prob - row_delta)).astype(jnp.bfloat16)
    score_total = jnp.sum(grad_scores.astype(jnp.float32), axis=0)
    table_part = jnp.einsum("hqk,qkb->bh", score_total, bucket_hot, precision=HIGHEST)
    grad_queries = (
        jnp.einsum("mhqk,mkhd->mqhd", grad_scores, key_rows, preferred_element_type=jnp.float32)
        * score_scale
    )
    grad_keys = (
        jnp.einsum("mhqk,mqhd->mkhd", grad_scores, queries, preferred_element_type=jnp.float32)
        * score_scale
    )
    grad_values = jnp.einsum(
        "mhqk,mqhd->mkhd",
        prob_again.astype(jnp.bfloat16),
        grad_context,
        preferred_element_type=jnp.float32,
    )
    grad_qkv = jnp.concatenate(
        [
            grad_queries.reshape(row_count, model_width),
            grad_keys.reshape(row_count, model_width),
            grad_values.reshape(row_count, model_width),
        ],
        axis=1,
    ).astype(jnp.bfloat16)
    out_grads, in_grads, grad_qkv = lax.optimization_barrier((out_grads, in_grads, grad_qkv))
    expert_in_grad = jnp.stack(in_grads)
    expert_out_grad = jnp.stack(out_grads)
    qkv_part = jnp.einsum("nc,nd->cd", normed_low, grad_qkv, preferred_element_type=jnp.float32)
    grad_normed = jnp.einsum("nd,cd->nc", grad_qkv, qkv_full, preferred_element_type=jnp.float32)
    grad_x_part, gain_attn_part = jax.vjp(rms_norm, flat_x, gain_attn)[1](grad_normed)
    tokens_grad = (grad_middle + grad_x_part).astype(jnp.bfloat16).reshape(tokens.shape)
    split = 3 * model_width // 2
    early = halving_scatter(jnp.concatenate([out_part, router_part], axis=1), sizes, orders[0])
    out_grad, router_grad = early[:, :model_width], early[:, model_width:]
    qkv_grad = jnp.concatenate(
        [
            halving_scatter(qkv_part[:, :split], sizes, orders[0]),
            halving_scatter(qkv_part[:, split:], sizes, orders[1]),
        ],
        axis=1,
    )
    small = butterfly_sum(
        jnp.concatenate([gain_attn_part, gain_ffn_part, table_part.reshape(-1)]), sizes
    )
    gain_attn_grad = small[:model_width]
    gain_ffn_grad = small[model_width : 2 * model_width]
    table_grad = small[2 * model_width :].reshape(bias_table.shape)
    return (
        block_out,
        tokens_grad,
        gain_attn_grad,
        qkv_grad,
        out_grad,
        table_grad,
        gain_ffn_grad,
        router_grad,
        expert_in_grad,
        expert_out_grad,
    )


def solution(mesh):
    sizes = {"dp": mesh.shape["dp"], "expert": mesh.shape["expert"]}
    return jax.shard_map(
        functools.partial(on_device, sizes),
        mesh=mesh,
        in_specs=(
            P(None, ("dp", "expert"), None),
            P(),
            P(("dp", "expert"), None),
            P(("dp", "expert"), None),
            P(),
            P(),
            P(("dp", "expert"), None),
            P("expert", None, "dp"),
            P("expert", "dp", None),
            P(None, ("dp", "expert"), None),
            P(),
            P(None, ("dp", "expert"), None),
            P(None, ("dp", "expert"), None),
        ),
        out_specs=(
            P(None, ("dp", "expert"), None),
            P(None, ("dp", "expert"), None),
            P(),
            P(("dp", "expert"), None),
            P(("dp", "expert"), None),
            P(),
            P(),
            P(("dp", "expert"), None),
            P("expert", None, "dp"),
            P("expert", "dp", None),
        ),
        check_vma=False,
    )
```
